512 devices in a mesh: det: 2 (over core), bank: 128 (over z, x_hi, y), seg: 2 (over x_lo).
Axes of the slice: x: 4 (x_hi: 2, x_lo: 2; x = x_hi * 2 + x_lo), y: 4, z: 16, core: 2. Of those that a mesh axis runs over, the one named last changes fastest.
Arguments:
- strain: bfloat16 [2, 2, 2048], P('det', 'seg', 'bank'), may hold values from -6 to 6
- basis_filters: bfloat16 [128, 512, 640], P('bank', None, 'seg'), may hold values from -0.25 to 0.25
- template_mix: bfloat16 [128, 640, 2, 512], P('bank', None, None, 'seg'), may hold values from -0.25 to 0.25
- basis_counts: int32 [128], P('bank'), may hold values from 200 to 600, as said below
- window_bins: int32 [65536], P(('bank', 'seg')), may hold values from 0 to 2
- time_slides: int32 [2], replicated, may hold values from 0 to 31
Outputs:
- coincident_snr: float32 [65536], P(('bank', 'seg'))
The draws below stay inside these ranges and needn't reach their ends.
Inputs may be any that keep to these rules, and one draw needn't show every extreme that they name: `basis_counts`: slots of a sub-bank from its count up to 640 are padding.
All inputs are finite; a program needn't handle non-finite values.
Results may differ from the reference program's by a relative error of at most 0.00067.
Values may be sent and summed in bfloat16 or wider, within the bound.
No kernel may reach another device: no remote copies, remote signals or barrier semaphores. Data moves between devices by JAX's collectives and lax.ppermute only.
A program may use at most 64 MiB of HBM per device.

```python
import jax
import jax.numpy as jnp
from jax import lax

FILT = 512
NBMAX = 640
TPL = 512
SEGLEN = 2048
BIN = 128
WMAX = 2
NDET = 2
BANKS = 128
TEMPLATES = 65536
NBALL = 32
N_SEG = 2


def draw_basis_counts(key, part):
    lowest = NBMAX * 5 // 16
    highest = NBMAX * 15 // 16
    first_key, second_key = jax.random.split(key)
    counted = jax.random.randint(first_key, (BANKS,), lowest, highest + 1, dtype=jnp.int32)
    shuffled = jax.random.permutation(second_key, BANKS)
    counted = counted.at[shuffled[0]].set(highest).at[shuffled[1]].set(lowest)
    return counted.astype(jnp.int32)


def touch_ends(entries, rng, low, largest):
    dims = entries.shape
    spot = [jax.random.randint(jax.random.fold_in(rng, axis), (), 0, dims[axis]) for axis in range(len(dims))]
    entries = entries.at[tuple(spot)].set(low)
    longest = dims.index(max(dims))
    spot[longest] = (spot[longest] + 1) % dims[longest]
    return entries.at[tuple(spot)].set(largest)


def levels(stream_key, shape, cuts, least, high):
    factor_of, own = 1.0, jax.random.fold_in(stream_key, 6)
    for dim, shards_of in cuts:
        steps = jnp.exp(jax.random.uniform(jax.random.fold_in(own, dim), (shards_of,), jnp.float32, least / len(cuts), high / len(cuts)))
        factor_of = factor_of * jnp.repeat(steps, shape[dim] // shards_of).reshape([-1 if axis == dim else 1 for axis in range(len(shape))])
    return factor_of


def noise(own_key, extent, width, most, pieces=(), kind=jnp.bfloat16):
    loudness = levels(own_key, extent, pieces, -0.22, 0.18) if pieces else 1.0
    entries = jax.random.normal(own_key, extent, jnp.float32) * width * loudness
    return jnp.minimum(jnp.maximum(entries, -most), most).astype(kind)


def setup_inputs(seed: int = 0) -> dict:
    keys = jax.random.split(jax.random.key(seed), 7)
    return {
        "strain": noise(keys[0], (NDET, N_SEG, SEGLEN), 1.0, 6.0, ((0, 2), (1, 2), (2, 128))),
        "basis_filters": noise(keys[1], (BANKS, FILT, NBMAX), FILT ** -0.5, 0.25, ((0, 128), (2, 2))),
        "template_mix": noise(keys[2], (BANKS, NBMAX, 2, TPL), NBMAX ** -0.5, 0.25, ((0, 128), (3, 2))),
        "basis_counts": draw_basis_counts(jax.random.fold_in(keys[6], 71), 0),
        "window_bins": touch_ends(jax.random.randint(keys[4], (TEMPLATES,), 0, WMAX + 1), jax.random.fold_in(keys[4], 1), 0, WMAX).astype(jnp.int32),
        "time_slides": jax.random.randint(keys[5], (NDET,), 0, NBALL).astype(jnp.int32),
    }


def correlate(samples, filter_bank):
    output = lax.conv_general_dilated(samples[None, :, None], filter_bank[:, None, :], (1,), 'VALID', dimension_numbers=('NWC', 'WIO', 'NWC'), preferred_element_type=jnp.float32)
    return output[0]

def reference(strain, basis_filters, template_mix, basis_counts, window_bins, time_slides):
    window_length = N_SEG * SEGLEN
    zero_tail = jnp.zeros((FILT - 1,), strain.dtype)

    def one_bank(operands):
        filter_bank, mixing, filter_count = operands
        in_use = jnp.arange(NBMAX, dtype=jnp.int32) < filter_count
        powers = []
        for detector in range(NDET):
            samples = jnp.concatenate([strain[detector].reshape(window_length), zero_tail])
            correlated = correlate(samples, filter_bank).astype(jnp.bfloat16)
            correlated = jnp.where(in_use[None, :], correlated, jnp.zeros((), jnp.bfloat16))
            complex_snr = jnp.dot(correlated, mixing.reshape(NBMAX, 2 * TPL), preferred_element_type=jnp.float32)
            snr_squared = complex_snr[:, :TPL] * complex_snr[:, :TPL] + complex_snr[:, TPL:] * complex_snr[:, TPL:]
            powers.append(lax.optimization_barrier(jnp.max(snr_squared.reshape(NBALL, BIN, TPL), axis=1)))
        return jnp.stack(powers)
    peak_power = lax.map(one_bank, (basis_filters, template_mix, basis_counts))
    first_det = jnp.roll(peak_power[:, 0], -time_slides[0], axis=1)
    second_det = jnp.roll(peak_power[:, 1], -time_slides[1], axis=1)
    limits = window_bins.reshape(BANKS, 1, TPL)
    best_power = second_det
    for offset in range(1, WMAX + 1):
        for direction in (1, -1):
            candidate = jnp.roll(second_det, -direction * offset, axis=1)
            best_power = jnp.maximum(best_power, jnp.where(limits >= offset, candidate, jnp.zeros((), jnp.float32)))
    return jnp.sqrt(lax.optimization_barrier(jnp.max(first_det + best_power, axis=1))).reshape(TEMPLATES)
```

```python
import jax
import jax.numpy as jnp
from jax import lax
from jax.experimental import pallas as pl
from jax.experimental.pallas import tpu as pltpu
from jax.sharding import Mesh, PartitionSpec as P

BIN = 128
WMAX = 2
LANES = 128
PLANE = ("det", "xh", "y", "seg")
BANK = ("z", "xh", "y")


def filters_kernel(count_ref, own_ref, other_ref, mix_ref, out_ref):
    seg = lax.axis_index("seg")
    det = lax.axis_index("det")
    half = own_ref.shape[0]
    width = out_ref.shape[1] // 2
    count = count_ref[0]
    columns = pl.ds(pl.multiple_of(det * width, LANES), width)
    for quad in range(2):
        total = None
        for place, filters in ((seg, own_ref), (1 - seg, other_ref)):
            first = pl.multiple_of(place * half, 64)
            coefs = mix_ref[quad, pl.ds(first, half), columns]
            slot = first + lax.broadcasted_iota(jnp.int32, coefs.shape, 0)
            coefs = jnp.where(slot < count, coefs.astype(jnp.float32), 0.0).astype(jnp.bfloat16)
            part = lax.dot_general(
                filters[...], coefs, (((0,), (0,)), ((), ())), preferred_element_type=jnp.float32
            )
            total = part if total is None else total + part
        out_ref[:, quad * width : (quad + 1) * width] = total.astype(jnp.bfloat16)


def peaks_kernel(slides_ref, pieces_ref, filt_ref, limits_ref, out_ref, hankel, power):
    n_pieces, n_z, _ = pieces_ref.shape
    fine = n_pieces // 4
    step = LANES // fine
    bins = 2 * n_z
    taps = filt_ref.shape[0]
    spans = taps // LANES
    width = filt_ref.shape[1] // 2
    row = lax.broadcasted_iota(jnp.int32, (BIN, LANES), 0)
    lane = lax.broadcasted_iota(jnp.int32, (BIN, LANES), 1)
    early = lane <= row
    filt = filt_ref[...]
    group = 8
    for det in range(2):
        rows = []
        for seg in range(2):
            total = None
            for piece in range(fine):
                samples = pieces_ref[(det * fine + piece) * 2 + seg].astype(jnp.float32)
                if piece:
                    samples = pltpu.roll(samples, piece * step, 1)
                total = samples if total is None else total + samples
            rows.append(total)
        series = jnp.concatenate(rows, axis=0)

        def turned(c):
            return pltpu.roll(
                jnp.broadcast_to(series[c : c + 1], (BIN, LANES)), 1, 1, stride=1, stride_axis=0
            )

        here = turned(0)
        for c in range(bins + spans - 1):
            after = turned(c + 1) if c + 1 < bins else jnp.zeros((BIN, LANES), jnp.float32)
            tile = jnp.where(early, here, after).astype(jnp.bfloat16)
            here = after
            for span in range(spans):
                if 0 <= c - span < bins:
                    hankel[pl.ds((c - span) * BIN, BIN), span * LANES : (span + 1) * LANES] = tile
        for first in range(0, bins, group):
            snr = jnp.dot(
                hankel[pl.ds(first * BIN, group * BIN), :], filt, preferred_element_type=jnp.float32
            )
            real, imag = snr[:, :width], snr[:, width:]
            squared = (real * real + imag * imag).reshape(group, BIN, width)
            peak = jnp.max(squared, axis=1)
            for copy in range(3):
                power[det, pl.ds(copy * bins + first, group), :] = peak

    which = lax.axis_index("det")
    limits = jnp.where(which == 0, limits_ref[0:1], limits_ref[1:2])
    first_det = power[0, pl.ds(bins + slides_ref[0], bins), :]
    best = power[1, pl.ds(bins + slides_ref[1], bins), :]
    for offset in range(1, WMAX + 1):
        for direction in (1, -1):
            moved = power[1, pl.ds(bins + slides_ref[1] + direction * offset, bins), :]
            best = jnp.maximum(best, jnp.where(limits >= offset, moved, 0.0))
    out_ref[...] = jnp.sqrt(jnp.max(first_det + best, axis=0, keepdims=True))


def shards(strain, basis_filters, template_mix, basis_counts, window_bins, time_slides):
    taps = basis_filters.shape[1]
    width = template_mix.shape[3] // 2
    n_z = lax.axis_size("z")
    n_plane = 1
    for axis in PLANE:
        n_plane *= lax.axis_size(axis)
    bins = lax.axis_size("seg") * n_z

    vmem = pl.BlockSpec(memory_space=pltpu.VMEM)
    smem = pl.BlockSpec(memory_space=pltpu.SMEM)

    own = jnp.transpose(basis_filters[0])
    other = lax.ppermute(own, "seg", [(0, 1), (1, 0)])

    piece = jnp.pad(strain[0, 0].astype(jnp.float32), (0, LANES - strain.shape[2]))
    along = lax.all_to_all(
        jnp.broadcast_to(piece[None, None], (n_z, 1, LANES)), "z", 0, 0, tiled=True
    )
    along = along.reshape(n_z, LANES).astype(jnp.bfloat16)
    pieces = lax.all_to_all(
        jnp.broadcast_to(along[None], (n_plane, n_z, LANES)), PLANE, 0, 0, tiled=True
    )

    mix = jnp.transpose(template_mix[0], (1, 0, 2))
    filt = pl.pallas_call(
        filters_kernel,
        out_shape=jax.ShapeDtypeStruct((taps, 2 * width), jnp.bfloat16),
        in_specs=[smem, vmem, vmem, vmem],
        out_specs=vmem,
        compiler_params=pltpu.CompilerParams(vmem_limit_bytes=24 << 20),
        cost_estimate=pl.CostEstimate(
            flops=4 * taps * width * mix.shape[1], bytes_accessed=2 << 20, transcendentals=0
        ),
    )(basis_counts, own, other, mix)
    mine = pl.pallas_call(
        peaks_kernel,
        out_shape=jax.ShapeDtypeStruct((1, width), jnp.float32),
        in_specs=[smem, vmem, vmem, vmem],
        out_specs=vmem,
        scratch_shapes=[
            pltpu.VMEM((bins * BIN, taps), jnp.bfloat16),
            pltpu.VMEM((2, 3 * bins, width), jnp.float32),
        ],
        compiler_params=pltpu.CompilerParams(vmem_limit_bytes=32 << 20),
    )(time_slides, pieces, filt, window_bins.reshape(2, width))
    return lax.all_gather(mine, "det", axis=0, tiled=True).reshape(2 * width)


def solution(mesh):
    n_det, n_bank, n_seg = mesh.devices.shape
    fine = Mesh(mesh.devices.reshape(n_det, n_bank // 8, 2, 4, n_seg), ("det", "z", "xh", "y", "seg"))
    placed = (
        P("det", "seg", BANK),
        P(BANK, None, "seg"),
        P(BANK, None, None, "seg"),
        P(BANK),
        P((*BANK, "seg")),
        P(),
    )
    return jax.shard_map(
        shards, mesh=fine, in_specs=placed, out_specs=P((*BANK, "seg")), check_vma=False
    )
```

```python
import jax
import jax.numpy as jnp
from jax import lax
from jax.experimental import pallas as pl
from jax.experimental.pallas import tpu as pltpu
from jax.sharding import Mesh, PartitionSpec as P

BIN = 128
WMAX = 2
FIRST_Z = 11
LANES = 128
CHIPS = ("xh", "y", "seg", "z")
BANK = ("z", "xh", "y")


def filters_kernel(count_ref, own_ref, other_ref, mix_ref, out_ref):
    seg = lax.axis_index("seg")
    half = own_ref.shape[0]
    width = mix_ref.shape[2]
    count = count_ref[0]
    for quad in range(2):
        total = None
        for place, filters in ((seg, own_ref), (1 - seg, other_ref)):
            first = pl.multiple_of(place * half, 64)
            coefs = mix_ref[quad, pl.ds(first, half), :]
            slot = first + lax.broadcasted_iota(jnp.int32, coefs.shape, 0)
            coefs = jnp.where(slot < count, coefs.astype(jnp.float32), 0.0).astype(jnp.bfloat16)
            part = lax.dot_general(
                filters[...], coefs, (((0,), (0,)), ((), ())), preferred_element_type=jnp.float32
            )
            total = part if total is None else total + part
        out_ref[:, quad * width : (quad + 1) * width] = total.astype(jnp.bfloat16)


def peaks_kernel(slides_ref, pieces_ref, filt_ref, limits_ref, out_ref, hankel, power):
    bins, width = out_ref.shape
    n_z = bins // 2
    fine = pieces_ref.shape[0] // bins
    step = LANES // fine
    taps = filt_ref.shape[0]
    spans = taps // LANES
    group = 4
    row = lax.broadcasted_iota(jnp.int32, (BIN, LANES), 0)
    lane = lax.broadcasted_iota(jnp.int32, (BIN, LANES), 1)
    early = lane <= row
    filt = filt_ref[...]
    series = None
    for piece in range(fine):
        rows = []
        for first in (piece * bins, piece * bins + n_z):
            mark = first + n_z - FIRST_Z
            rows += [pieces_ref[mark : first + n_z, :], pieces_ref[first:mark, :]]
        samples = jnp.concatenate(rows, axis=0)
        if piece:
            samples = pltpu.roll(samples, piece * step, 1)
        series = samples if series is None else series + samples

    def turned(c):
        return pltpu.roll(
            jnp.broadcast_to(series[c : c + 1], (BIN, LANES)), 1, 1, stride=1, stride_axis=0
        )

    here = turned(0)
    for c in range(bins + spans - 1):
        after = turned(c + 1) if c + 1 < bins else jnp.zeros((BIN, LANES), jnp.float32)
        tile = jnp.where(early, here, after).astype(jnp.bfloat16)
        here = after
        for span in range(spans):
            if 0 <= c - span < bins:
                hankel[pl.ds((c - span) * BIN, BIN), span * LANES : (span + 1) * LANES] = tile
    for first in range(0, bins, group):
        snr = jnp.dot(
            hankel[pl.ds(first * BIN, group * BIN), :], filt, preferred_element_type=jnp.float32
        )
        real, imag = snr[:, :width], snr[:, width:]
        squared = (real * real + imag * imag).reshape(group, BIN, width)
        peak = jnp.max(squared, axis=1)
        power[pl.ds(first, group), :] = peak

    det = lax.axis_index("det")
    limits = jnp.where(det == 0, 0, limits_ref[...])
    shifted = pltpu.roll(power[...], lax.rem(bins - slides_ref[det], bins), 0)
    best = shifted
    for offset in range(1, WMAX + 1):
        for turn in (offset, bins - offset):
            moved = pltpu.roll(shifted, turn, 0)
            best = jnp.maximum(best, jnp.where(limits >= offset, moved, 0.0))
    out_ref[...] = best


def shards(strain, basis_filters, template_mix, basis_counts, window_bins, time_slides):
    taps = basis_filters.shape[1]
    width = template_mix.shape[3]
    n_chips = 1
    for axis in CHIPS:
        n_chips *= lax.axis_size(axis)
    bins = lax.axis_size("seg") * lax.axis_size("z")

    vmem = pl.BlockSpec(memory_space=pltpu.VMEM)
    smem = pl.BlockSpec(memory_space=pltpu.SMEM)

    own = jnp.transpose(basis_filters[0])
    other = lax.ppermute(own, "seg", [(0, 1), (1, 0)])

    piece = jnp.pad(strain[0, 0].astype(jnp.float32), (0, LANES - strain.shape[2]))
    n_z = lax.axis_size("z")
    order = [c - c % n_z + (c + FIRST_Z) % n_z for c in range(n_chips)]
    pieces = lax.all_to_all(
        jnp.broadcast_to(piece[None, None], (n_chips, 1, LANES)),
        CHIPS,
        0,
        0,
        axis_index_groups=[order],
        tiled=True,
    ).reshape(n_chips, LANES)

    mix = jnp.transpose(template_mix[0], (1, 0, 2))
    filt = pl.pallas_call(
        filters_kernel,
        out_shape=jax.ShapeDtypeStruct((taps, 2 * width), jnp.bfloat16),
        in_specs=[smem, vmem, vmem, vmem],
        out_specs=vmem,
        compiler_params=pltpu.CompilerParams(vmem_limit_bytes=24 << 20),
        cost_estimate=pl.CostEstimate(
            flops=1 * 4 * taps * width * mix.shape[1], bytes_accessed=2 << 20, transcendentals=0
        ),
    )(basis_counts, own, other, mix)
    mine = pl.pallas_call(
        peaks_kernel,
        out_shape=jax.ShapeDtypeStruct((bins, width), jnp.float32),
        in_specs=[smem, vmem, vmem, vmem],
        out_specs=vmem,
        scratch_shapes=[
            pltpu.VMEM((bins * BIN, taps), jnp.bfloat16),
            pltpu.VMEM((bins, width), jnp.float32),
        ],
        compiler_params=pltpu.CompilerParams(vmem_limit_bytes=32 << 20),
    )(time_slides, pieces, filt, window_bins.reshape(1, width))
    both = lax.all_gather(mine, "det", axis=0, tiled=False)
    return jnp.sqrt(jnp.max(both[0] + both[1], axis=0))


def solution(mesh):
    n_det, n_bank, n_seg = mesh.devices.shape
    fine = Mesh(mesh.devices.reshape(n_det, n_bank // 8, 2, 4, n_seg), ("det", "z", "xh", "y", "seg"))
    placed = (
        P("det", "seg", BANK),
        P(BANK, None, "seg"),
        P(BANK, None, None, "seg"),
        P(BANK),
        P((*BANK, "seg")),
        P(),
    )
    return jax.shard_map(
        shards, mesh=fine, in_specs=placed, out_specs=P((*BANK, "seg")), check_vma=False
    )
```

```python
import jax
import jax.numpy as jnp
from jax import lax
from jax.experimental import pallas as pl
from jax.experimental.pallas import tpu as pltpu
from jax.sharding import Mesh, PartitionSpec as P

BIN = 128
WMAX = 2
LANES = 128
FIRST_Z = 11
CHIPS = ("xh", "y", "seg", "z")
BANK = ("z", "xh", "y")


def rows_kernel(count_ref, slides_ref, window_ref, counts_ref, limits_ref, turn_ref):
    det = lax.axis_index("det")
    bins = lax.axis_size("seg") * lax.axis_size("z")
    counts_ref[...] = jnp.full(counts_ref.shape, count_ref[0], jnp.int32)
    limits_ref[...] = jnp.where(det == 0, 0, window_ref[...])
    turn_ref[...] = jnp.full(turn_ref.shape, lax.rem(bins - slides_ref[det], bins), jnp.int32)


def filters_kernel(counts_ref, own_ref, other_ref, mix_ref, out_ref):
    seg = lax.axis_index("seg")
    half = own_ref.shape[0]
    width = mix_ref.shape[2]
    count = counts_ref[...]
    for quad in range(2):
        total = None
        for place, filters in ((seg, own_ref), (1 - seg, other_ref)):
            first = pl.multiple_of(place * half, 64)
            coefs = mix_ref[quad, pl.ds(first, half), :]
            slot = first + lax.broadcasted_iota(jnp.int32, coefs.shape, 0)
            coefs = jnp.where(slot < count, coefs.astype(jnp.float32), 0.0).astype(jnp.bfloat16)
            part = lax.dot_general(
                filters[...], coefs, (((0,), (0,)), ((), ())), preferred_element_type=jnp.float32
            )
            total = part if total is None else total + part
        out_ref[:, quad * width : (quad + 1) * width] = total.astype(jnp.bfloat16)


def peaks_kernel(turn_ref, pieces_ref, filt_ref, limits_ref, out_ref, hankel, power):
    bins, width = out_ref.shape
    n_z = bins // 2
    fine = pieces_ref.shape[0] // bins
    step = LANES // fine
    taps = filt_ref.shape[0]
    spans = taps // LANES
    group = 4
    row = lax.broadcasted_iota(jnp.int32, (BIN, LANES), 0)
    lane = lax.broadcasted_iota(jnp.int32, (BIN, LANES), 1)
    early = lane <= row
    filt = filt_ref[...]
    series = None
    for piece in range(fine):
        rows = []
        for first in (piece * bins, piece * bins + n_z):
            mark = first + n_z - FIRST_Z
            rows += [pieces_ref[mark : first + n_z, :], pieces_ref[first:mark, :]]
        samples = jnp.concatenate(rows, axis=0)
        if piece:
            samples = pltpu.roll(samples, piece * step, 1)
        series = samples if series is None else series + samples

    def turned(c):
        return pltpu.roll(
            jnp.broadcast_to(series[c : c + 1], (BIN, LANES)), 1, 1, stride=1, stride_axis=0
        )

    here = turned(0)
    made = 0
    for first in range(0, bins, group):
        while made < first + group + spans - 1:
            after = turned(made + 1) if made + 1 < bins else jnp.zeros((BIN, LANES), jnp.float32)
            tile = jnp.where(early, here, after).astype(jnp.bfloat16)
            here = after
            for span in range(spans):
                if 0 <= made - span < bins:
                    hankel[pl.ds((made - span) * BIN, BIN), span * LANES : (span + 1) * LANES] = tile
            made += 1
        snr = jnp.dot(
            hankel[pl.ds(first * BIN, group * BIN), :], filt, preferred_element_type=jnp.float32
        )
        real, imag = snr[:, :width], snr[:, width:]
        squared = (real * real + imag * imag).reshape(group, BIN, width)
        power[pl.ds(first, group), :] = jnp.max(squared, axis=1)

    limits = limits_ref[...]
    turn = turn_ref[...]
    shifted = power[...]
    for bit in range((bins - 1).bit_length()):
        moved = pltpu.roll(shifted, 1 << bit, 0)
        shifted = jnp.where(((turn >> bit) & 1) == 1, moved, shifted)
    best = shifted
    for offset in range(1, WMAX + 1):
        for step in (offset, bins - offset):
            moved = pltpu.roll(shifted, step, 0)
            best = jnp.maximum(best, jnp.where(limits >= offset, moved, 0.0))
    out_ref[...] = best


def shards(strain, basis_filters, template_mix, basis_counts, window_bins, time_slides):
    taps = basis_filters.shape[1]
    width = template_mix.shape[3]
    n_z = lax.axis_size("z")
    n_chips = 1
    for axis in CHIPS:
        n_chips *= lax.axis_size(axis)
    bins = lax.axis_size("seg") * n_z

    vmem = pl.BlockSpec(memory_space=pltpu.VMEM)
    smem = pl.BlockSpec(memory_space=pltpu.SMEM)

    own = jnp.transpose(basis_filters[0])
    other = lax.ppermute(own, "seg", [(0, 1), (1, 0)])

    order = [c - c % n_z + (c + FIRST_Z) % n_z for c in range(n_chips)]
    piece = jnp.pad(strain[0, 0].astype(jnp.float32), (0, LANES - strain.shape[2]))
    pieces = lax.all_to_all(
        jnp.broadcast_to(piece[None, None], (n_chips, 1, LANES)),
        CHIPS,
        0,
        0,
        axis_index_groups=[order],
        tiled=True,
    )
    pieces = pieces.reshape(n_chips, LANES)

    counts, limits, turn = pl.pallas_call(
        rows_kernel,
        out_shape=(pltpu.VMEM((1, width), jnp.int32),) * 3,
        in_specs=[smem, smem, vmem],
        out_specs=(vmem, vmem, vmem),
    )(basis_counts, time_slides, window_bins.reshape(1, width))
    mix = jnp.transpose(template_mix[0], (1, 0, 2))
    filt = pl.pallas_call(
        filters_kernel,
        out_shape=jax.ShapeDtypeStruct((taps, 2 * width), jnp.bfloat16),
        in_specs=[vmem, vmem, vmem, vmem],
        out_specs=vmem,
        compiler_params=pltpu.CompilerParams(vmem_limit_bytes=24 << 20),
        cost_estimate=pl.CostEstimate(
            flops=4 * taps * width * mix.shape[1], bytes_accessed=2 << 20, transcendentals=0
        ),
    )(counts, own, other, mix)
    mine = pl.pallas_call(
        peaks_kernel,
        out_shape=jax.ShapeDtypeStruct((bins, width), jnp.float32),
        in_specs=[vmem, vmem, vmem, vmem],
        out_specs=vmem,
        scratch_shapes=[
            pltpu.VMEM((bins * BIN, taps), jnp.bfloat16),
            pltpu.VMEM((bins, width), jnp.float32),
        ],
        compiler_params=pltpu.CompilerParams(vmem_limit_bytes=32 << 20),
    )(turn, pieces, filt, limits)
    both = lax.all_gather(mine, "det", axis=0, tiled=False)
    return jnp.sqrt(jnp.max(both[0] + both[1], axis=0))


def solution(mesh):
    n_det, n_bank, n_seg = mesh.devices.shape
    fine = Mesh(mesh.devices.reshape(n_det, n_bank // 8, 2, 4, n_seg), ("det", "z", "xh", "y", "seg"))
    placed = (
        P("det", "seg", BANK),
        P(BANK, None, "seg"),
        P(BANK, None, None, "seg"),
        P(BANK),
        P((*BANK, "seg")),
        P(),
    )
    return jax.shard_map(
        shards, mesh=fine, in_specs=placed, out_specs=P((*BANK, "seg")), check_vma=False
    )
```

```python
import jax
import jax.numpy as jnp
from jax import lax
from jax.experimental import pallas as pl
from jax.experimental.pallas import tpu as pltpu
from jax.sharding import Mesh, PartitionSpec as P

BIN = 128
WMAX = 2
LANES = 128
FIRST_Z = 11
CHIPS = ("xh", "y", "seg", "z")
BANK = ("z", "xh", "y")


def rows_kernel(count_ref, slides_ref, window_ref, counts_ref, limits_ref, turn_ref):
    det = lax.axis_index("det")
    bins = lax.axis_size("seg") * lax.axis_size("z")
    counts_ref[...] = jnp.full(counts_ref.shape, count_ref[0], jnp.int32)
    limits_ref[...] = jnp.where(det == 0, 0, window_ref[...])
    turn_ref[...] = jnp.full(turn_ref.shape, lax.rem(bins - slides_ref[det], bins), jnp.int32)


def filters_kernel(counts_ref, own_ref, other_ref, mix_ref, out_ref):
    seg = lax.axis_index("seg")
    half = own_ref.shape[0]
    width = mix_ref.shape[2]
    count = counts_ref[...]
    for quad in range(2):
        total = None
        for place, filters in ((seg, own_ref), (1 - seg, other_ref)):
            first = pl.multiple_of(place * half, 64)
            coefs = mix_ref[quad, pl.ds(first, half), :]
            slot = first + lax.broadcasted_iota(jnp.int32, coefs.shape, 0)
            coefs = jnp.where(slot < count, coefs.astype(jnp.float32), 0.0).astype(jnp.bfloat16)
            part = lax.dot_general(
                filters[...], coefs, (((0,), (0,)), ((), ())), preferred_element_type=jnp.float32
            )
            total = part if total is None else total + part
        out_ref[:, quad * width : (quad + 1) * width] = total.astype(jnp.bfloat16)


def peaks_kernel(turn_ref, pieces_ref, filt_ref, limits_ref, out_ref, hankel, power):
    bins, width = out_ref.shape
    n_z = bins // 2
    fine = pieces_ref.shape[0] // bins
    step = LANES // fine
    taps = filt_ref.shape[0]
    spans = taps // LANES
    group = 4
    row = lax.broadcasted_iota(jnp.int32, (BIN, LANES), 0)
    lane = lax.broadcasted_iota(jnp.int32, (BIN, LANES), 1)
    early = lane <= row
    filt = filt_ref[...]
    series = None
    for piece in range(fine):
        rows = []
        for first in (piece * bins, piece * bins + n_z):
            mark = first + n_z - FIRST_Z
            rows += [pieces_ref[mark : first + n_z, :], pieces_ref[first:mark, :]]
        samples = jnp.concatenate(rows, axis=0)
        if piece:
            samples = pltpu.roll(samples, piece * step, 1)
        series = samples if series is None else series + samples

    def turned(c):
        return pltpu.roll(
            jnp.broadcast_to(series[c : c + 1], (BIN, LANES)), 1, 1, stride=1, stride_axis=0
        )

    here = turned(0)
    made = 0
    for first in range(0, bins, group):
        while made < first + group + spans - 1:
            after = turned(made + 1) if made + 1 < bins else jnp.zeros((BIN, LANES), jnp.float32)
            tile = jnp.where(early, here, after).astype(jnp.bfloat16)
            here = after
            for span in range(spans):
                if 0 <= made - span < bins:
                    hankel[pl.ds((made - span) * BIN, BIN), span * LANES : (span + 1) * LANES] = tile
            made += 1
        snr = jnp.dot(
            hankel[pl.ds(first * BIN, group * BIN), :], filt, preferred_element_type=jnp.float32
        )
        real, imag = snr[:, :width], snr[:, width:]
        squared = (real * real + imag * imag).reshape(group, BIN, width)
        power[pl.ds(first, group), :] = jnp.max(squared, axis=1)

    limits = limits_ref[...]
    turn = turn_ref[...]
    shifted = power[...]
    for bit in range((bins - 1).bit_length()):
        moved = pltpu.roll(shifted, 1 << bit, 0)
        shifted = jnp.where(((turn >> bit) & 1) == 1, moved, shifted)
    best = shifted
    for offset in range(1, WMAX + 1):
        for step in (offset, bins - offset):
            moved = pltpu.roll(shifted, step, 0)
            best = jnp.maximum(best, jnp.where(limits >= offset, moved, 0.0))
    out_ref[...] = best


def shards(strain, basis_filters, template_mix, basis_counts, window_bins, time_slides):
    taps = basis_filters.shape[1]
    width = template_mix.shape[3]
    n_z = lax.axis_size("z")
    n_chips = 1
    for axis in CHIPS:
        n_chips *= lax.axis_size(axis)
    bins = lax.axis_size("seg") * n_z

    vmem = pl.BlockSpec(memory_space=pltpu.VMEM)
    smem = pl.BlockSpec(memory_space=pltpu.SMEM)

    own = jnp.transpose(basis_filters[0])
    part = own.shape[0] // lax.axis_size("det")
    fetched = lax.ppermute(
        lax.dynamic_slice_in_dim(own, lax.axis_index("det") * part, part, 0), "seg", [(0, 1), (1, 0)]
    )
    other = lax.all_gather(fetched, "det", axis=0, tiled=True)

    order = [c - c % n_z + (c + FIRST_Z) % n_z for c in range(n_chips)]
    piece = jnp.pad(strain[0, 0].astype(jnp.float32), (0, LANES - strain.shape[2]))
    pieces = lax.all_to_all(
        jnp.broadcast_to(piece[None, None], (n_chips, 1, LANES)),
        CHIPS,
        0,
        0,
        axis_index_groups=[order],
        tiled=True,
    )
    pieces = pieces.reshape(n_chips, LANES)

    counts, limits, turn = pl.pallas_call(
        rows_kernel,
        out_shape=(pltpu.VMEM((1, width), jnp.int32),) * 3,
        in_specs=[smem, smem, vmem],
        out_specs=(vmem, vmem, vmem),
    )(basis_counts, time_slides, window_bins.reshape(1, width))
    mix = jnp.transpose(template_mix[0], (1, 0, 2))
    filt = pl.pallas_call(
        filters_kernel,
        out_shape=jax.ShapeDtypeStruct((taps, 2 * width), jnp.bfloat16),
        in_specs=[vmem, vmem, vmem, vmem],
        out_specs=vmem,
        compiler_params=pltpu.CompilerParams(vmem_limit_bytes=24 << 20),
        cost_estimate=pl.CostEstimate(
            flops=1 * taps * width * mix.shape[1], bytes_accessed=2 << 20, transcendentals=0
        ),
    )(counts, own, other, mix)
    mine = pl.pallas_call(
        peaks_kernel,
        out_shape=jax.ShapeDtypeStruct((bins, width), jnp.float32),
        in_specs=[vmem, vmem, vmem, vmem],
        out_specs=vmem,
        scratch_shapes=[
            pltpu.VMEM((bins * BIN, taps), jnp.bfloat16),
            pltpu.VMEM((bins, width), jnp.float32),
        ],
        compiler_params=pltpu.CompilerParams(vmem_limit_bytes=32 << 20),
    )(turn, pieces, filt, limits)
    both = lax.all_gather(mine, "det", axis=0, tiled=False)
    return jnp.sqrt(jnp.max(both[0] + both[1], axis=0))


def solution(mesh):
    n_det, n_bank, n_seg = mesh.devices.shape
    fine = Mesh(mesh.devices.reshape(n_det, n_bank // 8, 2, 4, n_seg), ("det", "z", "xh", "y", "seg"))
    placed = (
        P("det", "seg", BANK),
        P(BANK, None, "seg"),
        P(BANK, None, None, "seg"),
        P(BANK),
        P((*BANK, "seg")),
        P(),
    )
    return jax.shard_map(
        shards, mesh=fine, in_specs=placed, out_specs=P((*BANK, "seg")), check_vma=False
    )
```
